32 devices in a mesh: expert: 4 (over y, x), dp: 4 (over z), mp: 2 (over core).
Axes of the slice: x: 2, y: 2, z: 4, core: 2. Of those that a mesh axis runs over, the one named last changes fastest.
Arguments:
- tokens: bfloat16 [6304, 768], P(('expert', 'dp', 'mp')), may hold values from -6 to 6
- cotangent: bfloat16 [6304, 768], P(('expert', 'dp', 'mp')), may hold values from -6 to 6
- routes: int32 [6304, 2], P(('expert', 'dp', 'mp')), may hold values from 0 to 3, all different within a row
- norm1_gain: float32 [768], replicated, may hold values from 0.5 to 1.5
- norm1_shift: float32 [768], replicated, may hold values from -1 to 1
- attn_input: bfloat16 [768, 3, 768], P('dp', None, 'mp'), may hold values from -0.21875 to 0.21875
- input_bias: float32 [2, 768], replicated, may hold values from -1 to 1
- attn_output: bfloat16 [768, 768], P('dp', 'mp'), may hold values from -0.875 to 0.875
- output_bias: float32 [768], replicated, may hold values from -1 to 1
- norm2_gain: float32 [768], replicated, may hold values from 0.5 to 1.5
- norm2_shift: float32 [768], replicated, may hold values from -1 to 1
- router_weight: bfloat16 [768, 4], replicated, may hold values from -0.15625 to 0.15625
- up_weight: bfloat16 [4, 768, 3072], P('expert', None, ('dp', 'mp')), may hold values from -0.21875 to 0.21875
- up_bias: bfloat16 [4, 3072], P('expert', ('dp', 'mp')), may hold values from -0.8984375 to 0.8984375
- down_weight: bfloat16 [4, 3072, 768], P('expert', ('dp', 'mp')), may hold values from -0.4375 to 0.4375
- down_bias: bfloat16 [4, 768], P('expert', ('dp', 'mp')), may hold values from -6 to 6
Outputs:
- mixed: bfloat16 [6304, 768], P(('expert', 'dp', 'mp'))
- tokens_grad: float32 [6304, 768], P(('expert', 'dp', 'mp'))
- norm1_gain_grad: float32 [768], replicated
- norm1_shift_grad: float32 [768], replicated
- attn_input_grad: float32 [768, 3, 768], P('dp', None, 'mp')
- input_bias_grad: float32 [2, 768], replicated
- attn_output_grad: float32 [768, 768], P('dp', 'mp')
- output_bias_grad: float32 [768], replicated
- norm2_gain_grad: float32 [768], replicated
- norm2_shift_grad: float32 [768], replicated
- router_grad: float32 [768, 4], replicated
- up_weight_grad: float32 [4, 768, 3072], P('expert', None, ('dp', 'mp'))
- up_bias_grad: float32 [4, 3072], P('expert', ('dp', 'mp'))
- down_weight_grad: float32 [4, 3072, 768], P('expert', ('dp', 'mp'))
- down_bias_grad: float32 [4, 768], P('expert', ('dp', 'mp'))
The draws below stay inside these ranges and needn't reach their ends.
Inputs may be any that keep to these rules, and one draw needn't show every extreme that they name: `routes`: each row names two different experts.
All inputs are finite; a program needn't handle non-finite values.
Results may differ from the reference program's by a relative error of at most 0.017.
Values may be sent and summed in bfloat16 or wider, within the bound.
A program may use at most 128 MiB of HBM per device.

```python
from functools import partial
import jax
import jax.numpy as jnp
from jax import lax

D = 768
HEADS = 12
HEAD_DIM = 64
FF = 3072
SEQ = 197
EXPERTS = 4
IMAGES = 32
TOKENS = 6304
ROWS = 197
CAP = 98
N_EXPERT = 4
N_DP = 4
N_MP = 2


def shard_levels(key, dims, pieces, low, high):
    factor_of, own = 1.0, jax.random.fold_in(key, 6)
    for dim, blocks in pieces:
        heights = jnp.exp(jax.random.uniform(jax.random.fold_in(own, dim), (blocks,), jnp.float32, low / len(pieces), high / len(pieces)))
        factor_of = factor_of * jnp.repeat(heights, dims[dim] // blocks).reshape([-1 if axis == dim else 1 for axis in range(len(dims))])
    return factor_of


def distinct(own_key, rows, number_of, top, lift):
    sequence = jax.random.permutation(jax.random.fold_in(own_key, 1), number_of)
    pull = sequence
    for power in range(3):
        pull = pull * pull // number_of
    pull = pull * lift // number_of
    lots = jax.random.randint(jax.random.fold_in(own_key, 2), (rows, number_of), 0, 4096) + pull
    sure = jax.random.permutation(jax.random.fold_in(own_key, 3), rows)[jnp.arange(number_of) % rows]
    lots = jnp.where(jnp.arange(rows)[:, None] == sure[None, :], 1 << 14, lots)
    priority = lots * number_of + jnp.arange(number_of)
    return lax.top_k(priority.astype(jnp.int32), top)[1].astype(jnp.int32)


def bell_draw(stream_key, shape, scale, limit, cuts=(), kind=jnp.bfloat16):
    level = shard_levels(stream_key, shape, cuts, -0.22, 0.18) if cuts else 1.0
    values = jax.random.normal(stream_key, shape, jnp.float32) * scale * level
    return jnp.minimum(jnp.maximum(values, -limit), limit).astype(kind)


def setup_inputs(seed: int = 0) -> dict:
    streams_of = jax.random.split(jax.random.key(seed), 17)
    return {
        "tokens": bell_draw(streams_of[0], (TOKENS, D), 1.0, 6.0, ((0, 32),)),
        "cotangent": bell_draw(streams_of[1], (TOKENS, D), 1.0, 6.0, ((0, 32),)),
        "routes": distinct(streams_of[2], TOKENS, EXPERTS, 2, 4096),
        "norm1_gain": jnp.clip(1.0 + 0.1 * jax.random.normal(streams_of[3], (D,), jnp.float32), 0.5, 1.5),
        "norm1_shift": bell_draw(streams_of[4], (D,), 0.2, 1.0, (), jnp.float32),
        "attn_input": bell_draw(streams_of[5], (D, 3, D), D ** -0.5, 0.21875, ((0, 4), (2, 2))),
        "input_bias": bell_draw(streams_of[6], (2, D), 0.2, 1.0, (), jnp.float32),
        "attn_output": bell_draw(streams_of[7], (D, D), (D // 16) ** -0.5, 0.875, ((0, 4), (1, 2))),
        "output_bias": bell_draw(streams_of[8], (D,), 0.2, 1.0, (), jnp.float32),
        "norm2_gain": jnp.clip(1.0 + 0.1 * jax.random.normal(streams_of[9], (D,), jnp.float32), 0.5, 1.5),
        "norm2_shift": bell_draw(streams_of[10], (D,), 0.2, 1.0, (), jnp.float32),
        "router_weight": bell_draw(streams_of[11], (D, EXPERTS), (2 * D) ** -0.5, 0.15625),
        "up_weight": bell_draw(streams_of[12], (EXPERTS, D, FF), D ** -0.5, 0.21875, ((0, 4), (2, 8))),
        "up_bias": bell_draw(streams_of[13], (EXPERTS, FF), 0.15, 0.8984375, ((0, 4), (1, 8))),
        "down_weight": bell_draw(streams_of[14], (EXPERTS, FF, D), (max(FF // (EXPERTS * EXPERTS), 1)) ** -0.5, 0.4375, ((0, 4), (1, 8))),
        "down_bias": bell_draw(streams_of[15], (EXPERTS, D), 1.0, 6.0, ((0, 4), (1, 8))),
    }


@jax.custom_vjp
def low(v):
    return lax.optimization_barrier(v.astype(jnp.bfloat16)).astype(jnp.float32)

@jax.custom_vjp
def low_back(v):
    return v

def low_keep(v):
    return (low(v), None)

def low_pass(kept, grad):
    return (grad,)

def back_keep(v):
    return (v, None)

def back_low(kept, grad):
    return (low(grad),)
low.defvjp(low_keep, low_pass)
low_back.defvjp(back_keep, back_low)
epsilon = 1e-06
highest = lax.Precision.HIGHEST

def layer_norm(values, norm_gain, norm_shift):
    center = values - lax.optimization_barrier(jnp.mean(values, axis=-1, keepdims=True))
    spread = lax.optimization_barrier(jnp.mean(center * center, axis=-1, keepdims=True))
    return center * lax.rsqrt(spread + epsilon) * norm_gain + norm_shift

def slot_plan(route_rows):
    flat_routes = jnp.concatenate([route_rows[:, 0], route_rows[:, 1]]).astype(jnp.int32)
    expert_ids = jnp.arange(EXPERTS, dtype=jnp.int32)
    one_hot = (flat_routes[:, None] == expert_ids[None, :]).astype(jnp.int32)
    earlier = jnp.cumsum(one_hot, axis=0) - one_hot
    position = lax.optimization_barrier(jnp.sum(earlier * one_hot, axis=1))
    return jnp.where(position < CAP, flat_routes * CAP + position, EXPERTS * CAP).astype(jnp.int32)

def attend_block(image_block, norm1_gain, norm1_shift, attn_input, input_bias, attn_output):
    image_count = image_block.shape[0]
    normed = low(layer_norm(image_block, norm1_gain, norm1_shift))
    project = jnp.einsum('isd,dkf->iskf', normed, attn_input, precision=highest)
    head_shape = (image_count, SEQ, HEADS, HEAD_DIM)
    queries = low(low_back(project[:, :, 0] + input_bias[0])).reshape(head_shape)
    keys_heads = low(low_back(project[:, :, 1])).reshape(head_shape)
    values_heads = low(low_back(project[:, :, 2] + input_bias[1])).reshape(head_shape)
    scores = jnp.einsum('iqhe,ikhe->ihqk', queries, keys_heads, precision=highest) * HEAD_DIM ** (-0.5)
    scores = low_back(scores)
    weights = low(jax.nn.softmax(scores, axis=-1))
    mixed_heads = jnp.einsum('ihqk,ikhe->iqhe', weights, values_heads, precision=highest)
    mixed_heads = low(low_back(mixed_heads.reshape(image_count, SEQ, D)))
    return low_back(jnp.einsum('isf,df->isd', mixed_heads, attn_output, precision=highest))

def expert_apply(operands):
    slab_rows, up_weight, up_bias, down_weight, down_bias = operands
    before_act = low_back(jnp.dot(slab_rows, up_weight, precision=highest) + up_bias)
    hidden = low(jax.nn.gelu(before_act, approximate=False))
    return low(low_back(jnp.dot(hidden, down_weight, precision=highest) + down_bias))

def forward(routes, tokens, norm1_gain, norm1_shift, attn_input, input_bias, attn_output, output_bias, norm2_gain, norm2_shift, router_weight, up_weight, up_bias, down_weight, down_bias):
    device_count = N_EXPERT * N_DP * N_MP
    blocks = tokens.reshape(N_EXPERT, IMAGES // N_EXPERT, SEQ, D)
    attend = jax.checkpoint(attend_block)

    def attend_step(carried, image_block):
        return (carried, attend(image_block, norm1_gain, norm1_shift, attn_input, input_bias, attn_output))
    _, branch = lax.scan(attend_step, None, blocks)
    residual = tokens + branch.reshape(TOKENS, D) + output_bias

    def prepare(rows_in, route_rows):
        normed = low(layer_norm(rows_in, norm2_gain, norm2_shift))
        logits = jnp.dot(normed, router_weight, precision=highest)
        gates_all = jax.nn.softmax(logits, axis=-1)
        expert_ids = jnp.arange(EXPERTS, dtype=jnp.int32)
        gate_first = lax.optimization_barrier(jnp.sum(jnp.where(route_rows[:, 0:1] == expert_ids[None, :], gates_all, 0.0), axis=-1, keepdims=True))
        gate_second = lax.optimization_barrier(jnp.sum(jnp.where(route_rows[:, 1:2] == expert_ids[None, :], gates_all, 0.0), axis=-1, keepdims=True))
        target = slot_plan(route_rows)
        sent_rows = jnp.concatenate([low_back(normed), low_back(normed)], axis=0)
        buffer = jnp.zeros((EXPERTS * CAP + 1, D), sent_rows.dtype).at[target].add(sent_rows)
        return (buffer[:EXPERTS * CAP], gate_first, gate_second, target)
    buffers, gate_first, gate_second, targets = jax.vmap(prepare)(residual.reshape(device_count, ROWS, D), routes.reshape(device_count, ROWS, 2))
    slab_rows = buffers.reshape(device_count, EXPERTS, CAP, D).transpose(1, 0, 2, 3).reshape(EXPERTS, device_count * CAP, D)
    outputs = lax.map(jax.checkpoint(expert_apply), (slab_rows, up_weight, up_bias, down_weight, down_bias))
    outputs = outputs.reshape(EXPERTS, device_count, CAP, D).transpose(1, 0, 2, 3).reshape(device_count, EXPERTS * CAP, D)

    def combine(slot_rows, target, weight_first, weight_second):
        padded = jnp.concatenate([slot_rows, jnp.zeros((1, D), slot_rows.dtype)], axis=0)
        picked = padded[target]
        return weight_first * picked[:ROWS] + weight_second * picked[ROWS:]
    mixture = jax.vmap(combine)(outputs, targets, gate_first, gate_second)
    return residual + mixture.reshape(TOKENS, D)

def reference(tokens, cotangent, routes, norm1_gain, norm1_shift, attn_input, input_bias, attn_output, output_bias, norm2_gain, norm2_shift, router_weight, up_weight, up_bias, down_weight, down_bias):
    single = jnp.float32
    result, pullback = jax.vjp(partial(forward, routes), tokens.astype(single), norm1_gain, norm1_shift, attn_input.astype(single), input_bias, attn_output.astype(single), output_bias, norm2_gain, norm2_shift, router_weight.astype(single), up_weight.astype(single), up_bias.astype(single), down_weight.astype(single), down_bias.astype(single))
    tokens_grad, norm1_gain_grad, norm1_shift_grad, attn_input_grad, input_bias_grad, attn_output_grad, output_bias_grad, norm2_gain_grad, norm2_shift_grad, router_grad, up_weight_grad, up_bias_grad, down_weight_grad, down_bias_grad = pullback(cotangent.astype(single))
    return (result.astype(jnp.bfloat16), tokens_grad, norm1_gain_grad, norm1_shift_grad, attn_input_grad, input_bias_grad, attn_output_grad, output_bias_grad, norm2_gain_grad, norm2_shift_grad, router_grad, up_weight_grad, up_bias_grad, down_weight_grad, down_bias_grad)
```

```python
import jax
import jax.numpy as jnp
from jax import lax
from jax.sharding import PartitionSpec as P

HEAD_DIM = 64
EPSILON = 1e-06
BF = jnp.bfloat16
F32 = jnp.float32


def mm(spec, a, b):
    return jnp.einsum(spec, a, b, preferred_element_type=F32)


def norm_stats(values):
    center = values - jnp.mean(values, axis=-1, keepdims=True)
    inverse = lax.rsqrt(jnp.mean(center * center, axis=-1, keepdims=True) + EPSILON)
    return center * inverse, inverse


def norm_pull(xhat, inverse, gain, upstream):
    u = upstream * gain
    mean_u = jnp.mean(u, axis=-1, keepdims=True)
    mean_ux = jnp.mean(u * xhat, axis=-1, keepdims=True)
    return (u - mean_u - xhat * mean_ux) * inverse


def swap(value):
    return lax.ppermute(value, "mp", [(0, 1), (1, 0)])


def line_gather(shard, count, index):
    left, right = [shard], [shard]
    for k in range(1, count):
        left.append(
            lax.ppermute(left[-1], "dp", [(z, z - 1) for z in range(1, count - k + 1)])
        )
        right.append(
            lax.ppermute(right[-1], "dp", [(z, z + 1) for z in range(k - 1, count - 1)])
        )
    return [shard] + [
        jnp.where(index + k < count, left[k], right[count - k]) for k in range(1, count)
    ]


def to_owner(chunk, k, count):
    return lax.ppermute(chunk, "dp", [(z, (z + k) % count) for z in range(count)])


def attend(project, bias, heads):
    images, seq = project.shape[0], project.shape[1]
    shape = (images, seq, heads, HEAD_DIM)
    width = heads * HEAD_DIM
    q = (project[:, :, :width] + bias[0]).astype(BF).reshape(shape)
    k = project[:, :, width : 2 * width].astype(BF).reshape(shape)
    v = (project[:, :, 2 * width :] + bias[1]).astype(BF).reshape(shape)
    scores = mm("iqhe,ikhe->ihqk", q, k) * HEAD_DIM ** (-0.5)
    probs = jax.nn.softmax(scores, axis=-1)
    mixed = mm("ihqk,ikhe->iqhe", probs.astype(BF), v).astype(BF)
    return (q, k, v, probs), mixed.reshape(images, seq, width)


def attend_back(kept, grad_mixed):
    q, k, v, probs = kept
    grad_mixed = grad_mixed.reshape(q.shape)
    scale = HEAD_DIM ** (-0.5)
    grad_v = mm("ihqk,iqhe->ikhe", probs.astype(BF), grad_mixed)
    grad_probs = mm("iqhe,ikhe->ihqk", grad_mixed, v)
    grad_scores = (
        probs * (grad_probs - jnp.sum(probs * grad_probs, axis=-1, keepdims=True))
    ).astype(BF)
    grad_q = mm("ihqk,ikhe->iqhe", grad_scores, k) * scale
    grad_k = mm("ihqk,iqhe->ikhe", grad_scores, q) * scale
    images, seq = q.shape[:2]
    return jnp.concatenate(
        [g.astype(BF).reshape(images, seq, -1) for g in (grad_q, grad_k, grad_v)], axis=-1
    )


def on_device(
    tokens, cotangent, routes, norm1_gain, norm1_shift, attn_input, input_bias, attn_output,
    output_bias, norm2_gain, norm2_shift, router_weight, up_weight, up_bias, down_weight, down_bias,
):
    rows, width = tokens.shape
    local = attn_input.shape[2]
    heads = local // HEAD_DIM
    mp_index, dp_index = lax.axis_index("mp"), lax.axis_index("dp")
    expert_index = lax.axis_index("expert")
    mp_count, dp_count = lax.axis_size("mp"), lax.axis_size("dp")
    expert_axis = lax.axis_size("expert")
    experts = router_weight.shape[1]
    capacity = 2 * rows // experts
    padded = -(-capacity // 8) * 8
    slots = experts * padded

    shard = jnp.concatenate(
        [attn_input.reshape(attn_input.shape[0], 3 * local), attn_output], axis=1
    )
    part = shard.shape[0] // expert_axis
    mine = lax.dynamic_slice_in_dim(shard, expert_index * part, part, 0)
    attn_full = lax.all_gather(mine, ("dp", "expert"), axis=0, tiled=True)
    input_full, output_full = attn_full[:, : 3 * local], attn_full[:, 3 * local :]

    other_tokens = swap(tokens)
    ff_part = up_weight.shape[2]
    bias_part = down_bias.shape[1]
    ups = line_gather(up_weight[0], dp_count, dp_index)
    downs = line_gather(down_weight[0], dp_count, dp_index)
    bias_own = jnp.concatenate([up_bias, down_bias], axis=1)
    biases = [bias_own] + [to_owner(bias_own, dp_count - k, dp_count) for k in range(1, dp_count)]

    flat_routes = jnp.concatenate([routes[:, 0], routes[:, 1]])
    expert_ids = jnp.arange(experts, dtype=jnp.int32)
    one_hot = flat_routes[:, None] == expert_ids[None, :]
    order = jnp.arange(2 * rows, dtype=jnp.int32)
    before = (order[:, None] > order[None, :]).astype(BF)
    earlier = mm("ab,be->ae", before, one_hot.astype(BF))
    position = jnp.sum(jnp.where(one_hot, earlier, 0.0), axis=1).astype(jnp.int32)
    target = jnp.where(position < capacity, flat_routes * padded + position, slots)
    place = (target[:, None] == jnp.arange(slots, dtype=jnp.int32)[None, :]).astype(BF)
    place_both = place[:rows] + place[rows:]

    pair = jnp.stack([tokens, other_tokens]).astype(F32)
    xhat1, inverse1 = norm_stats(pair)
    normed = (xhat1 * norm1_gain + norm1_shift).astype(BF)
    local_bias = lax.dynamic_slice_in_dim(input_bias, mp_index * local, local, 1)
    project = mm("itd,df->itf", normed, input_full)
    kept, mixed_heads = attend(project, local_bias, heads)
    from_other = swap(mm("tf,df->td", mixed_heads[1], output_full))
    residual = (
        tokens.astype(F32) + mm("tf,df->td", mixed_heads[0], output_full) + from_other + output_bias
    )

    xhat2, inverse2 = norm_stats(residual)
    routed = (xhat2 * norm2_gain + norm2_shift).astype(BF)
    gates_all = jax.nn.softmax(mm("td,de->te", routed, router_weight), axis=-1)
    pick_first, pick_second = one_hot[:rows], one_hot[rows:]
    gate_first = jnp.sum(jnp.where(pick_first, gates_all, 0.0), axis=-1, keepdims=True)
    gate_second = jnp.sum(jnp.where(pick_second, gates_all, 0.0), axis=-1, keepdims=True)
    upstream = cotangent.astype(F32)
    route_grads = jnp.concatenate([gate_first * upstream, gate_second * upstream]).astype(BF)
    send = jnp.concatenate(
        [
            mm("ts,td->sd", place_both, routed).astype(BF),
            mm("ts,td->sd", place, route_grads).astype(BF),
        ],
        axis=1,
    ).reshape(experts, padded, 2 * width)
    received = lax.all_to_all(send, "expert", split_axis=0, concat_axis=0, tiled=True)
    received = received.reshape(-1, 2 * width)
    count = received.shape[0]
    both = jnp.concatenate([received, swap(received)], axis=0)
    slab, slab_grad = both[:, :width], both[:, width:]

    produced = grad_slab = 0.0
    up_sums, down_sums, bias_sums = [], [], []
    column_sum = jnp.sum(slab_grad, axis=0, dtype=F32).reshape(dp_count, mp_count, bias_part)
    column_sum = lax.dynamic_index_in_dim(column_sum, mp_index, 1, keepdims=False)
    bias_row = jnp.zeros((dp_count, mp_count, bias_part), F32)
    for k in range(dp_count):
        owner = lax.rem(dp_index + k, dp_count)
        bias_k = biases[k].astype(F32)
        bias_row = lax.dynamic_update_slice(
            bias_row, bias_k[:, None, ff_part:], (owner, mp_index, jnp.int32(0))
        )
        pre = mm("td,df->tf", slab, ups[k]) + bias_k[:, :ff_part]
        cdf = 0.5 * (1.0 + lax.erf(pre * (0.5**0.5)))
        slope = cdf + pre * (jnp.exp(-0.5 * pre * pre) * 0.3989422804014327)
        hidden = (pre * cdf).astype(BF)
        produced = produced + mm("tf,fd->td", hidden, downs[k])
        grad_pre = (mm("td,fd->tf", slab_grad, downs[k]) * slope).astype(BF)
        grad_slab = grad_slab + mm("tf,df->td", grad_pre, ups[k])
        down_part = mm("tf,td->fd", hidden, slab_grad)
        up_part = mm("td,tf->df", slab, grad_pre)
        bias_grad = jnp.concatenate(
            [
                jnp.sum(grad_pre, axis=0, dtype=F32)[None, :],
                lax.dynamic_index_in_dim(column_sum, owner, 0),
            ],
            axis=1,
        )
        if k:
            down_part = to_owner(down_part.astype(BF), k, dp_count).astype(F32)
            up_part = to_owner(up_part.astype(BF), k, dp_count).astype(F32)
            bias_grad = to_owner(bias_grad, k, dp_count)
        down_sums.append(down_part)
        up_sums.append(up_part)
        bias_sums.append(bias_grad)
    produced = produced + bias_row.reshape(1, -1)
    partial = jnp.concatenate([produced, grad_slab], axis=1)
    back = (partial[:count] + swap(partial[count:].astype(BF)).astype(F32)).astype(BF)
    returned = lax.all_to_all(
        back.reshape(expert_axis, -1, 2 * width), "expert", split_axis=0, concat_axis=0, tiled=True
    ).reshape(slots, 2 * width)

    pick_one = mm("ts,sd->td", place[:rows], returned[:, :width])
    pick_two = mm("ts,sd->td", place[rows:], returned[:, :width])
    result = (residual + gate_first * pick_one + gate_second * pick_two).astype(BF)
    grad_first = jnp.sum(upstream * pick_one, axis=-1, keepdims=True)
    grad_second = jnp.sum(upstream * pick_two, axis=-1, keepdims=True)
    grad_gates = jnp.where(pick_first, grad_first, 0.0) + jnp.where(pick_second, grad_second, 0.0)
    grad_logits = gates_all * (grad_gates - jnp.sum(grad_gates * gates_all, axis=-1, keepdims=True))
    high = lax.Precision.HIGHEST
    router_grad = jnp.dot(routed.astype(F32).T, grad_logits, precision=high)
    grad_routed = jnp.dot(grad_logits, router_weight.astype(F32).T, precision=high)
    grad_routed = grad_routed + mm("ts,sd->td", place_both, returned[:, width:])
    grad_residual = upstream + norm_pull(xhat2, inverse2, norm2_gain, grad_routed)

    grad_branch = grad_residual.astype(BF)
    pair_grad = jnp.stack([grad_branch, swap(grad_branch)])
    grad_mixed = mm("itd,df->itf", pair_grad, output_full).astype(BF)
    output_grad = mm("itd,itf->df", pair_grad, mixed_heads)
    grad_project = attend_back(kept, grad_mixed)
    from_other = swap(mm("tf,df->td", grad_project[1], input_full).astype(BF))
    input_grad = mm("itd,itf->df", normed, grad_project)
    grad_normed = mm("tf,df->td", grad_project[0], input_full) + from_other.astype(F32)
    xhat_own, inverse_own = xhat1[0], inverse1[0]
    tokens_grad = grad_residual + norm_pull(xhat_own, inverse_own, norm1_gain, grad_normed)

    attn_grad = jnp.concatenate([input_grad, output_grad], axis=1).astype(BF)
    attn_grad = lax.psum_scatter(attn_grad, ("dp", "expert"), scatter_dimension=0, tiled=True)
    attn_grad = lax.all_gather(attn_grad, "expert", axis=0, tiled=True).astype(F32)

    bias_local = jnp.sum(grad_project, axis=(0, 1), dtype=F32)
    bias_local = jnp.stack([bias_local[:local], bias_local[2 * local :]])
    bias_full = lax.dynamic_update_slice_in_dim(
        jnp.zeros((2, width), F32), bias_local, mp_index * local, 1
    )
    small = jnp.concatenate(
        [
            jnp.sum(grad_normed * xhat_own, axis=0)[None],
            jnp.sum(grad_normed, axis=0)[None],
            bias_full,
            jnp.sum(grad_residual, axis=0)[None],
            jnp.sum(grad_routed * xhat2, axis=0)[None],
            jnp.sum(grad_routed, axis=0)[None],
            router_grad.T,
        ]
    )
    small = lax.psum(small, ("expert", "dp", "mp"))
    bias_total = sum(bias_sums)
    return (
        result,
        tokens_grad,
        small[0],
        small[1],
        attn_grad[:, : 3 * local].reshape(-1, 3, local),
        small[2:4],
        attn_grad[:, 3 * local :],
        small[4],
        small[5],
        small[6],
        small[7:].T,
        sum(up_sums)[None],
        bias_total[:, :ff_part],
        sum(down_sums)[None],
        bias_total[:, ff_part:],
    )


def solution(mesh):
    token_spec = P(("expert", "dp", "mp"), None)
    return jax.shard_map(
        on_device,
        mesh=mesh,
        in_specs=(
            token_spec, token_spec, token_spec, P(), P(), P("dp", None, "mp"), P(), P("dp", "mp"),
            P(), P(), P(), P(), P("expert", None, ("dp", "mp")), P("expert", ("dp", "mp")),
            P("expert", ("dp", "mp"), None), P("expert", ("dp", "mp")),
        ),
        out_specs=(
            token_spec, token_spec, P(), P(), P("dp", None, "mp"), P(), P("dp", "mp"),
            P(), P(), P(), P(), P("expert", None, ("dp", "mp")), P("expert", ("dp", "mp")),
            P("expert", ("dp", "mp"), None), P("expert", ("dp", "mp")),
        ),
        check_vma=False,
    )
```

```python
import jax
import jax.numpy as jnp
from jax import lax
from jax.sharding import PartitionSpec as P

HEAD_DIM = 64
EPSILON = 1e-06
BF = jnp.bfloat16
F32 = jnp.float32


def mm(spec, a, b):
    return jnp.einsum(spec, a, b, preferred_element_type=F32)


def norm_stats(values):
    center = values - jnp.mean(values, axis=-1, keepdims=True)
    inverse = lax.rsqrt(jnp.mean(center * center, axis=-1, keepdims=True) + EPSILON)
    return center * inverse, inverse


def norm_pull(xhat, inverse, gain, upstream):
    u = upstream * gain
    mean_u = jnp.mean(u, axis=-1, keepdims=True)
    mean_ux = jnp.mean(u * xhat, axis=-1, keepdims=True)
    return (u - mean_u - xhat * mean_ux) * inverse


def swap(value):
    return lax.ppermute(value, "mp", [(0, 1), (1, 0)])


def from_axis(shard, count):
    return [shard] + [to_owner(shard, count - k, count) for k in range(1, count)]


def across(value, j, count):
    return lax.ppermute(value, "expert", [(e, e ^ j) for e in range(count)])


def sum_all(value):
    for axis in ("mp", "expert", "dp"):
        count, step = lax.axis_size(axis), 1
        while step < count:
            value = value + lax.ppermute(value, axis, [(i, i ^ step) for i in range(count)])
            step *= 2
    return value


def to_owner(chunk, k, count):
    return lax.ppermute(chunk, "dp", [(z, (z + k) % count) for z in range(count)])


def attend(project, bias, heads):
    images, seq = project.shape[0], project.shape[1]
    shape = (images, seq, heads, HEAD_DIM)
    width = heads * HEAD_DIM
    q = (project[:, :, :width] + bias[0]).astype(BF).reshape(shape)
    k = project[:, :, width : 2 * width].astype(BF).reshape(shape)
    v = (project[:, :, 2 * width :] + bias[1]).astype(BF).reshape(shape)
    scores = mm("iqhe,ikhe->ihqk", q, k) * HEAD_DIM ** (-0.5)
    probs = jax.nn.softmax(scores, axis=-1)
    mixed = mm("ihqk,ikhe->iqhe", probs.astype(BF), v).astype(BF)
    return (q, k, v, probs), mixed.reshape(images, seq, width)


def attend_back(kept, grad_mixed):
    q, k, v, probs = kept
    grad_mixed = grad_mixed.reshape(q.shape)
    scale = HEAD_DIM ** (-0.5)
    grad_v = mm("ihqk,iqhe->ikhe", probs.astype(BF), grad_mixed)
    grad_probs = mm("iqhe,ikhe->ihqk", grad_mixed, v)
    grad_scores = (
        probs * (grad_probs - jnp.sum(probs * grad_probs, axis=-1, keepdims=True))
    ).astype(BF)
    grad_q = mm("ihqk,ikhe->iqhe", grad_scores, k) * scale
    grad_k = mm("ihqk,iqhe->ikhe", grad_scores, q) * scale
    images, seq = q.shape[:2]
    return jnp.concatenate(
        [g.astype(BF).reshape(images, seq, -1) for g in (grad_q, grad_k, grad_v)], axis=-1
    )


def on_device(
    tokens, cotangent, routes, norm1_gain, norm1_shift, attn_input, input_bias, attn_output,
    output_bias, norm2_gain, norm2_shift, router_weight, up_weight, up_bias, down_weight, down_bias,
):
    rows, width = tokens.shape
    local = attn_input.shape[2]
    heads = local // HEAD_DIM
    mp_index, dp_index = lax.axis_index("mp"), lax.axis_index("dp")
    expert_index = lax.axis_index("expert")
    mp_count, dp_count = lax.axis_size("mp"), lax.axis_size("dp")
    expert_axis = lax.axis_size("expert")
    experts = router_weight.shape[1]
    capacity = 2 * rows // experts
    padded = -(-capacity // 8) * 8
    slots = experts * padded

    shard = jnp.concatenate(
        [attn_input.reshape(attn_input.shape[0], 3 * local), attn_output], axis=1
    )
    part = shard.shape[0] // expert_axis
    mine = lax.dynamic_slice_in_dim(shard, expert_index * part, part, 0)
    column = jnp.stack(from_axis(mine, dp_count))
    column, up_own, down_own = lax.optimization_barrier((column, up_weight[0], down_weight[0]))
    column = lax.dynamic_slice_in_dim(
        jnp.concatenate([column, column]), lax.rem(dp_count - dp_index, dp_count), dp_count, 0
    )
    attn_full = jnp.zeros((dp_count, expert_axis) + mine.shape, BF)
    for j in range(expert_axis):
        piece = across(column, j, expert_axis) if j else column
        attn_full = lax.dynamic_update_slice(
            attn_full, piece[:, None], (0, expert_index ^ j, 0, 0)
        )
    attn_full = attn_full.reshape(width, 4 * local)
    input_full, output_full = attn_full[:, : 3 * local], attn_full[:, 3 * local :]

    other_tokens = swap(tokens)
    ff_part = up_weight.shape[2]
    bias_part = down_bias.shape[1]
    ups = from_axis(up_own, dp_count)
    downs = from_axis(down_own, dp_count)
    bias_own = jnp.concatenate([up_bias, down_bias], axis=1)
    biases = from_axis(bias_own, dp_count)

    flat_routes = jnp.concatenate([routes[:, 0], routes[:, 1]])
    expert_ids = jnp.arange(experts, dtype=jnp.int32)
    one_hot = flat_routes[:, None] == expert_ids[None, :]
    order = jnp.arange(2 * rows, dtype=jnp.int32)
    before = (order[:, None] > order[None, :]).astype(BF)
    earlier = mm("ab,be->ae", before, one_hot.astype(BF))
    position = jnp.sum(jnp.where(one_hot, earlier, 0.0), axis=1).astype(jnp.int32)
    target = jnp.where(position < capacity, flat_routes * padded + position, slots)
    place = (target[:, None] == jnp.arange(slots, dtype=jnp.int32)[None, :]).astype(BF)
    place_both = place[:rows] + place[rows:]

    pair = jnp.stack([tokens, other_tokens]).astype(F32)
    xhat1, inverse1 = norm_stats(pair)
    normed = (xhat1 * norm1_gain + norm1_shift).astype(BF)
    local_bias = lax.dynamic_slice_in_dim(input_bias, mp_index * local, local, 1)
    project = mm("itd,df->itf", normed, input_full)
    kept, mixed_heads = attend(project, local_bias, heads)
    from_other = swap(mm("tf,df->td", mixed_heads[1], output_full))
    residual = (
        tokens.astype(F32) + mm("tf,df->td", mixed_heads[0], output_full) + from_other + output_bias
    )

    xhat2, inverse2 = norm_stats(residual)
    routed = (xhat2 * norm2_gain + norm2_shift).astype(BF)
    gates_all = jax.nn.softmax(mm("td,de->te", routed, router_weight), axis=-1)
    pick_first, pick_second = one_hot[:rows], one_hot[rows:]
    gate_first = jnp.sum(jnp.where(pick_first, gates_all, 0.0), axis=-1, keepdims=True)
    gate_second = jnp.sum(jnp.where(pick_second, gates_all, 0.0), axis=-1, keepdims=True)
    upstream = cotangent.astype(F32)
    route_grads = jnp.concatenate([gate_first * upstream, gate_second * upstream]).astype(BF)
    send = jnp.concatenate(
        [
            mm("ts,td->sd", place_both, routed).astype(BF),
            mm("ts,td->sd", place, route_grads).astype(BF),
        ],
        axis=1,
    ).reshape(experts, padded, 2 * width)
    received = lax.all_to_all(send, "expert", split_axis=0, concat_axis=0, tiled=True)
    received = received.reshape(-1, 2 * width)
    count = received.shape[0]
    both = jnp.concatenate([received, swap(received)], axis=0)
    slab, slab_grad = both[:, :width], both[:, width:]

    produced = grad_slab = 0.0
    up_sums, down_sums, bias_sums = [], [], []
    column_sum = jnp.sum(slab_grad, axis=0, dtype=F32).reshape(dp_count, mp_count, bias_part)
    column_sum = lax.dynamic_index_in_dim(column_sum, mp_index, 1, keepdims=False)
    bias_row = jnp.zeros((dp_count, mp_count, bias_part), F32)
    for k in range(dp_count):
        owner = lax.rem(dp_index + k, dp_count)
        bias_k = biases[k].astype(F32)
        bias_row = lax.dynamic_update_slice(
            bias_row, bias_k[:, None, ff_part:], (owner, mp_index, jnp.int32(0))
        )
        pre = mm("td,df->tf", slab, ups[k]) + bias_k[:, :ff_part]
        cdf = 0.5 * (1.0 + lax.erf(pre * (0.5**0.5)))
        slope = cdf + pre * (jnp.exp(-0.5 * pre * pre) * 0.3989422804014327)
        hidden = (pre * cdf).astype(BF)
        produced = produced + mm("tf,fd->td", hidden, downs[k])
        grad_pre = (mm("td,fd->tf", slab_grad, downs[k]) * slope).astype(BF)
        grad_slab = grad_slab + mm("tf,df->td", grad_pre, ups[k])
        down_part = mm("tf,td->fd", hidden, slab_grad)
        up_part = mm("td,tf->df", slab, grad_pre)
        bias_grad = jnp.concatenate(
            [
                jnp.sum(grad_pre, axis=0, dtype=F32)[None, :],
                lax.dynamic_index_in_dim(column_sum, owner, 0),
            ],
            axis=1,
        )
        if k:
            down_part = to_owner(down_part.astype(BF), k, dp_count).astype(F32)
            up_part = to_owner(up_part.astype(BF), k, dp_count).astype(F32)
            bias_grad = to_owner(bias_grad, k, dp_count)
        down_sums.append(down_part)
        up_sums.append(up_part)
        bias_sums.append(bias_grad)
    produced = produced + bias_row.reshape(1, -1)
    partial = jnp.concatenate([produced, grad_slab], axis=1)
    back = (partial[:count] + swap(partial[count:].astype(BF)).astype(F32)).astype(BF)
    returned = lax.all_to_all(
        back.reshape(expert_axis, -1, 2 * width), "expert", split_axis=0, concat_axis=0, tiled=True
    ).reshape(slots, 2 * width)

    pick_one = mm("ts,sd->td", place[:rows], returned[:, :width])
    pick_two = mm("ts,sd->td", place[rows:], returned[:, :width])
    result = (residual + gate_first * pick_one + gate_second * pick_two).astype(BF)
    grad_first = jnp.sum(upstream * pick_one, axis=-1, keepdims=True)
    grad_second = jnp.sum(upstream * pick_two, axis=-1, keepdims=True)
    grad_gates = jnp.where(pick_first, grad_first, 0.0) + jnp.where(pick_second, grad_second, 0.0)
    grad_logits = gates_all * (grad_gates - jnp.sum(grad_gates * gates_all, axis=-1, keepdims=True))
    high = lax.Precision.HIGHEST
    router_grad = jnp.dot(routed.astype(F32).T, grad_logits, precision=high)
    grad_routed = jnp.dot(grad_logits, router_weight.astype(F32).T, precision=high)
    grad_routed = grad_routed + mm("ts,sd->td", place_both, returned[:, width:])
    grad_residual = upstream + norm_pull(xhat2, inverse2, norm2_gain, grad_routed)

    grad_branch = grad_residual.astype(BF)
    pair_grad = jnp.stack([grad_branch, swap(grad_branch)])
    grad_mixed = mm("itd,df->itf", pair_grad, output_full).astype(BF)
    output_grad = mm("itd,itf->df", pair_grad, mixed_heads)
    grad_project = attend_back(kept, grad_mixed)
    from_other = swap(mm("tf,df->td", grad_project[1], input_full).astype(BF))
    input_grad = mm("itd,itf->df", normed, grad_project)
    grad_normed = mm("tf,df->td", grad_project[0], input_full) + from_other.astype(F32)
    xhat_own, inverse_own = xhat1[0], inverse1[0]
    tokens_grad = grad_residual + norm_pull(xhat_own, inverse_own, norm1_gain, grad_normed)

    attn_grad = jnp.concatenate([input_grad, output_grad], axis=1).astype(BF)
    attn_grad = attn_grad.reshape(dp_count, expert_axis, part, 4 * local)
    quarter = 0.0
    for j in range(expert_axis):
        piece = lax.dynamic_index_in_dim(attn_grad, expert_index ^ j, 1, keepdims=False)
        quarter = quarter + (across(piece, j, expert_axis) if j else piece).astype(F32)
    quarter = quarter.astype(BF)
    share = 0.0
    for k in range(dp_count):
        piece = lax.dynamic_index_in_dim(
            quarter, lax.rem(dp_index + k, dp_count), 0, keepdims=False
        )
        share = share + (to_owner(piece, k, dp_count) if k else piece).astype(F32)
    share = share.astype(BF)
    attn_grad = jnp.zeros((expert_axis,) + share.shape, F32)
    for j in range(expert_axis):
        piece = (across(share, j, expert_axis) if j else share).astype(F32)
        attn_grad = lax.dynamic_update_slice(attn_grad, piece[None], (expert_index ^ j, 0, 0))
    attn_grad = attn_grad.reshape(-1, 4 * local)

    bias_local = jnp.sum(grad_project, axis=(0, 1), dtype=F32)
    bias_local = jnp.stack([bias_local[:local], bias_local[2 * local :]])
    bias_full = lax.dynamic_update_slice_in_dim(
        jnp.zeros((2, width), F32), bias_local, mp_index * local, 1
    )
    small = jnp.concatenate(
        [
            jnp.sum(grad_normed * xhat_own, axis=0)[None],
            jnp.sum(grad_normed, axis=0)[None],
            bias_full,
            jnp.sum(grad_residual, axis=0)[None],
            jnp.sum(grad_routed * xhat2, axis=0)[None],
            jnp.sum(grad_routed, axis=0)[None],
            router_grad.T,
        ]
    )
    small = sum_all(small)
    bias_total = sum(bias_sums)
    return (
        result,
        tokens_grad,
        small[0],
        small[1],
        attn_grad[:, : 3 * local].reshape(-1, 3, local),
        small[2:4],
        attn_grad[:, 3 * local :],
        small[4],
        small[5],
        small[6],
        small[7:].T,
        sum(up_sums)[None],
        bias_total[:, :ff_part],
        sum(down_sums)[None],
        bias_total[:, ff_part:],
    )


def solution(mesh):
    token_spec = P(("expert", "dp", "mp"), None)
    return jax.shard_map(
        on_device,
        mesh=mesh,
        in_specs=(
            token_spec, token_spec, token_spec, P(), P(), P("dp", None, "mp"), P(), P("dp", "mp"),
            P(), P(), P(), P(), P("expert", None, ("dp", "mp")), P("expert", ("dp", "mp")),
            P("expert", ("dp", "mp"), None), P("expert", ("dp", "mp")),
        ),
        out_specs=(
            token_spec, token_spec, P(), P(), P("dp", None, "mp"), P(), P("dp", "mp"),
            P(), P(), P(), P(), P("expert", None, ("dp", "mp")), P("expert", ("dp", "mp")),
            P("expert", ("dp", "mp"), None), P("expert", ("dp", "mp")),
        ),
        check_vma=False,
    )
```

```python
import jax
import jax.numpy as jnp
from jax import lax
from jax.sharding import PartitionSpec as P

HEAD_DIM = 64
EPSILON = 1e-06
BF = jnp.bfloat16
F32 = jnp.float32


def mm(spec, a, b):
    return jnp.einsum(spec, a, b, preferred_element_type=F32)


def norm_stats(values):
    center = values - jnp.mean(values, axis=-1, keepdims=True)
    inverse = lax.rsqrt(jnp.mean(center * center, axis=-1, keepdims=True) + EPSILON)
    return center * inverse, inverse


def norm_pull(xhat, inverse, gain, upstream):
    u = upstream * gain
    mean_u = jnp.mean(u, axis=-1, keepdims=True)
    mean_ux = jnp.mean(u * xhat, axis=-1, keepdims=True)
    return (u - mean_u - xhat * mean_ux) * inverse


def swap(value):
    return lax.ppermute(value, "mp", [(0, 1), (1, 0)])


def from_axis(shard, count):
    return [shard] + [to_owner(shard, count - k, count) for k in range(1, count)]


def across(value, j, count):
    return lax.ppermute(value, "expert", [(e, e ^ j) for e in range(count)])


def sum_all(value):
    for axis in ("mp", "expert", "dp"):
        count, step = lax.axis_size(axis), 1
        while step < count:
            value = value + lax.ppermute(value, axis, [(i, i ^ step) for i in range(count)])
            step *= 2
    return value


def to_owner(chunk, k, count):
    return lax.ppermute(chunk, "dp", [(z, (z + k) % count) for z in range(count)])


def attend(project, bias, heads):
    images, seq = project.shape[0], project.shape[1]
    shape = (images, seq, heads, HEAD_DIM)
    width = heads * HEAD_DIM
    q = (project[:, :, :width] + bias[0]).astype(BF).reshape(shape)
    k = project[:, :, width : 2 * width].astype(BF).reshape(shape)
    v = (project[:, :, 2 * width :] + bias[1]).astype(BF).reshape(shape)
    scores = mm("iqhe,ikhe->ihqk", q, k) * HEAD_DIM ** (-0.5)
    probs = jax.nn.softmax(scores, axis=-1)
    mixed = mm("ihqk,ikhe->iqhe", probs.astype(BF), v).astype(BF)
    return (q, k, v, probs), mixed.reshape(images, seq, width)


def attend_back(kept, grad_mixed):
    q, k, v, probs = kept
    grad_mixed = grad_mixed.reshape(q.shape)
    scale = HEAD_DIM ** (-0.5)
    grad_v = mm("ihqk,iqhe->ikhe", probs.astype(BF), grad_mixed)
    grad_probs = mm("iqhe,ikhe->ihqk", grad_mixed, v)
    grad_scores = (
        probs * (grad_probs - jnp.sum(probs * grad_probs, axis=-1, keepdims=True))
    ).astype(BF)
    grad_q = mm("ihqk,ikhe->iqhe", grad_scores, k) * scale
    grad_k = mm("ihqk,iqhe->ikhe", grad_scores, q) * scale
    images, seq = q.shape[:2]
    return jnp.concatenate(
        [g.astype(BF).reshape(images, seq, -1) for g in (grad_q, grad_k, grad_v)], axis=-1
    )


def on_device(
    tokens, cotangent, routes, norm1_gain, norm1_shift, attn_input, input_bias, attn_output,
    output_bias, norm2_gain, norm2_shift, router_weight, up_weight, up_bias, down_weight, down_bias,
):
    rows, width = tokens.shape
    local = attn_input.shape[2]
    heads = local // HEAD_DIM
    mp_index, dp_index = lax.axis_index("mp"), lax.axis_index("dp")
    expert_index = lax.axis_index("expert")
    mp_count, dp_count = lax.axis_size("mp"), lax.axis_size("dp")
    expert_axis = lax.axis_size("expert")
    experts = router_weight.shape[1]
    capacity = 2 * rows // experts
    padded = -(-capacity // 8) * 8
    slots = experts * padded

    shard = jnp.concatenate(
        [attn_input.reshape(attn_input.shape[0], 3 * local), attn_output], axis=1
    )
    part = shard.shape[0] // expert_axis
    mine = lax.dynamic_slice_in_dim(shard, expert_index * part, part, 0)
    ff_part = up_weight.shape[2]
    bias_part = down_bias.shape[1]
    bias_own = jnp.concatenate([up_bias, down_bias], axis=1)
    bias_own = jnp.pad(bias_own, ((0, 7), (0, 4 * local - ff_part - bias_part)))
    column = jnp.stack(from_axis(jnp.concatenate([mine, bias_own]), dp_count))
    column = lax.dynamic_slice_in_dim(
        jnp.concatenate([column, column]), lax.rem(dp_count - dp_index, dp_count), dp_count, 0
    )
    up_bias_row = column[:, part, :ff_part].astype(F32).reshape(1, -1)
    down_bias_row = column[:, part, ff_part : ff_part + bias_part].astype(F32)
    column = column[:, :part]
    up_full = lax.all_gather(up_weight[0], "dp", axis=1, tiled=True)
    down_full = lax.all_gather(down_weight[0], "dp", axis=0, tiled=True)
    attn_full = jnp.zeros((dp_count, expert_axis) + mine.shape, BF)
    for j in range(expert_axis):
        piece = across(column, j, expert_axis) if j else column
        attn_full = lax.dynamic_update_slice(
            attn_full, piece[:, None], (0, expert_index ^ j, 0, 0)
        )
    attn_full = attn_full.reshape(width, 4 * local)
    input_full, output_full = attn_full[:, : 3 * local], attn_full[:, 3 * local :]

    other_tokens = swap(tokens)
    flat_routes = jnp.concatenate([routes[:, 0], routes[:, 1]])
    expert_ids = jnp.arange(experts, dtype=jnp.int32)
    one_hot = flat_routes[:, None] == expert_ids[None, :]
    order = jnp.arange(2 * rows, dtype=jnp.int32)
    before = (order[:, None] > order[None, :]).astype(BF)
    earlier = mm("ab,be->ae", before, one_hot.astype(BF))
    position = jnp.sum(jnp.where(one_hot, earlier, 0.0), axis=1).astype(jnp.int32)
    target = jnp.where(position < capacity, flat_routes * padded + position, slots)
    place = (target[:, None] == jnp.arange(slots, dtype=jnp.int32)[None, :]).astype(BF)
    place_both = place[:rows] + place[rows:]

    pair = jnp.stack([tokens, other_tokens]).astype(F32)
    xhat1, inverse1 = norm_stats(pair)
    normed = (xhat1 * norm1_gain + norm1_shift).astype(BF)
    local_bias = lax.dynamic_slice_in_dim(input_bias, mp_index * local, local, 1)
    project = mm("itd,df->itf", normed, input_full)
    kept, mixed_heads = attend(project, local_bias, heads)
    from_other = swap(mm("tf,df->td", mixed_heads[1], output_full))
    residual = (
        tokens.astype(F32) + mm("tf,df->td", mixed_heads[0], output_full) + from_other + output_bias
    )

    xhat2, inverse2 = norm_stats(residual)
    routed = (xhat2 * norm2_gain + norm2_shift).astype(BF)
    gates_all = jax.nn.softmax(mm("td,de->te", routed, router_weight), axis=-1)
    pick_first, pick_second = one_hot[:rows], one_hot[rows:]
    gate_first = jnp.sum(jnp.where(pick_first, gates_all, 0.0), axis=-1, keepdims=True)
    gate_second = jnp.sum(jnp.where(pick_second, gates_all, 0.0), axis=-1, keepdims=True)
    upstream = cotangent.astype(F32)
    route_grads = jnp.concatenate([gate_first * upstream, gate_second * upstream]).astype(BF)
    send = jnp.concatenate(
        [
            mm("ts,td->sd", place_both, routed).astype(BF),
            mm("ts,td->sd", place, route_grads).astype(BF),
        ],
        axis=1,
    ).reshape(experts, padded, 2 * width)
    received = lax.all_to_all(send, "expert", split_axis=0, concat_axis=0, tiled=True)
    received = received.reshape(-1, 2 * width)
    count = received.shape[0]
    both = jnp.concatenate([received, swap(received)], axis=0)
    slab, slab_grad = both[:, :width], both[:, width:]

    pre = mm("td,df->tf", slab, up_full) + up_bias_row
    cdf = 0.5 * (1.0 + lax.erf(pre * (0.5**0.5)))
    slope = cdf + pre * (jnp.exp(-0.5 * pre * pre) * 0.3989422804014327)
    hidden = (pre * cdf).astype(BF)
    bias_row = lax.dynamic_update_slice_in_dim(
        jnp.zeros((dp_count, mp_count, bias_part), F32), down_bias_row[:, None], mp_index, 1
    )
    produced = mm("tf,fd->td", hidden, down_full) + bias_row.reshape(1, -1)
    grad_pre = (mm("td,fd->tf", slab_grad, down_full) * slope).astype(BF)
    grad_slab = mm("tf,df->td", grad_pre, up_full)
    down_grad = mm("tf,td->fd", hidden, slab_grad).reshape(dp_count, ff_part, width)
    up_grad = mm("tf,td->fd", grad_pre, slab).reshape(dp_count, ff_part, width)
    column_sum = jnp.sum(slab_grad, axis=0, dtype=F32).reshape(dp_count, mp_count, bias_part)
    bias_grad = jnp.concatenate(
        [
            jnp.sum(grad_pre, axis=0, dtype=F32).reshape(dp_count, ff_part),
            lax.dynamic_index_in_dim(column_sum, mp_index, 1, keepdims=False),
        ],
        axis=1,
    )
    bias_grad = jnp.pad(
        bias_grad[:, None], ((0, 0), (0, 7), (0, width - ff_part - bias_part))
    )
    payload = jnp.concatenate([g.astype(BF) for g in (down_grad, up_grad, bias_grad)], axis=1)
    expert_grad = lax.psum_scatter(
        payload.reshape(-1, width), "dp", scatter_dimension=0, tiled=True
    ).astype(F32)
    partial = jnp.concatenate([produced, grad_slab], axis=1)
    back = (partial[:count] + swap(partial[count:].astype(BF)).astype(F32)).astype(BF)
    returned = lax.all_to_all(
        back.reshape(expert_axis, -1, 2 * width), "expert", split_axis=0, concat_axis=0, tiled=True
    ).reshape(slots, 2 * width)

    pick_one = mm("ts,sd->td", place[:rows], returned[:, :width])
    pick_two = mm("ts,sd->td", place[rows:], returned[:, :width])
    result = (residual + gate_first * pick_one + gate_second * pick_two).astype(BF)
    grad_first = jnp.sum(upstream * pick_one, axis=-1, keepdims=True)
    grad_second = jnp.sum(upstream * pick_two, axis=-1, keepdims=True)
    grad_gates = jnp.where(pick_first, grad_first, 0.0) + jnp.where(pick_second, grad_second, 0.0)
    grad_logits = gates_all * (grad_gates - jnp.sum(grad_gates * gates_all, axis=-1, keepdims=True))
    high = lax.Precision.HIGHEST
    router_grad = jnp.dot(routed.astype(F32).T, grad_logits, precision=high)
    grad_routed = jnp.dot(grad_logits, router_weight.astype(F32).T, precision=high)
    grad_routed = grad_routed + mm("ts,sd->td", place_both, returned[:, width:])
    grad_residual = upstream + norm_pull(xhat2, inverse2, norm2_gain, grad_routed)

    grad_branch = grad_residual.astype(BF)
    pair_grad = jnp.stack([grad_branch, swap(grad_branch)])
    grad_mixed = mm("itd,df->itf", pair_grad, output_full).astype(BF)
    output_grad = mm("itd,itf->df", pair_grad, mixed_heads)
    grad_project = attend_back(kept, grad_mixed)
    from_other = swap(mm("tf,df->td", grad_project[1], input_full).astype(BF))
    input_grad = mm("itd,itf->df", normed, grad_project)
    grad_normed = mm("tf,df->td", grad_project[0], input_full) + from_other.astype(F32)
    xhat_own, inverse_own = xhat1[0], inverse1[0]
    tokens_grad = grad_residual + norm_pull(xhat_own, inverse_own, norm1_gain, grad_normed)

    attn_grad = jnp.concatenate([input_grad, output_grad], axis=1).astype(BF)
    attn_grad = attn_grad.reshape(dp_count, expert_axis, part, 4 * local)
    quarter = 0.0
    for j in range(expert_axis):
        piece = lax.dynamic_index_in_dim(attn_grad, expert_index ^ j, 1, keepdims=False)
        quarter = quarter + (across(piece, j, expert_axis) if j else piece).astype(F32)
    quarter = quarter.astype(BF)
    share = 0.0
    for k in range(dp_count):
        piece = lax.dynamic_index_in_dim(
            quarter, lax.rem(dp_index + k, dp_count), 0, keepdims=False
        )
        share = share + (to_owner(piece, k, dp_count) if k else piece).astype(F32)
    share = share.astype(BF)
    attn_grad = jnp.zeros((expert_axis,) + share.shape, F32)
    for j in range(expert_axis):
        piece = (across(share, j, expert_axis) if j else share).astype(F32)
        attn_grad = lax.dynamic_update_slice(attn_grad, piece[None], (expert_index ^ j, 0, 0))
    attn_grad = attn_grad.reshape(-1, 4 * local)

    bias_local = jnp.sum(grad_project, axis=(0, 1), dtype=F32)
    bias_local = jnp.stack([bias_local[:local], bias_local[2 * local :]])
    bias_full = lax.dynamic_update_slice_in_dim(
        jnp.zeros((2, width), F32), bias_local, mp_index * local, 1
    )
    small = jnp.concatenate(
        [
            jnp.sum(grad_normed * xhat_own, axis=0)[None],
            jnp.sum(grad_normed, axis=0)[None],
            bias_full,
            jnp.sum(grad_residual, axis=0)[None],
            jnp.sum(grad_routed * xhat2, axis=0)[None],
            jnp.sum(grad_routed, axis=0)[None],
            router_grad.T,
        ]
    )
    small = sum_all(small)
    bias_total = expert_grad[2 * ff_part :][:1]
    return (
        result,
        tokens_grad,
        small[0],
        small[1],
        attn_grad[:, : 3 * local].reshape(-1, 3, local),
        small[2:4],
        attn_grad[:, 3 * local :],
        small[4],
        small[5],
        small[6],
        small[7:].T,
        expert_grad[ff_part : 2 * ff_part].T[None],
        bias_total[:, :ff_part],
        expert_grad[None, :ff_part],
        bias_total[:, ff_part : ff_part + bias_part],
    )


def solution(mesh):
    token_spec = P(("expert", "dp", "mp"), None)
    return jax.shard_map(
        on_device,
        mesh=mesh,
        in_specs=(
            token_spec, token_spec, token_spec, P(), P(), P("dp", None, "mp"), P(), P("dp", "mp"),
            P(), P(), P(), P(), P("expert", None, ("dp", "mp")), P("expert", ("dp", "mp")),
            P("expert", ("dp", "mp"), None), P("expert", ("dp", "mp")),
        ),
        out_specs=(
            token_spec, token_spec, P(), P(), P("dp", None, "mp"), P(), P("dp", "mp"),
            P(), P(), P(), P(), P("expert", None, ("dp", "mp")), P("expert", ("dp", "mp")),
            P("expert", ("dp", "mp"), None), P("expert", ("dp", "mp")),
        ),
        check_vma=False,
    )
```

```python
import jax
import jax.numpy as jnp
from jax import lax
from jax.sharding import PartitionSpec as P

HEAD_DIM = 64
EPSILON = 1e-06
BF = jnp.bfloat16
F32 = jnp.float32


def mm(spec, a, b):
    return jnp.einsum(spec, a, b, preferred_element_type=F32)


def norm_stats(values):
    center = values - jnp.mean(values, axis=-1, keepdims=True)
    inverse = lax.rsqrt(jnp.mean(center * center, axis=-1, keepdims=True) + EPSILON)
    return center * inverse, inverse


def norm_pull(xhat, inverse, gain, upstream):
    u = upstream * gain
    mean_u = jnp.mean(u, axis=-1, keepdims=True)
    mean_ux = jnp.mean(u * xhat, axis=-1, keepdims=True)
    return (u - mean_u - xhat * mean_ux) * inverse


def swap(value):
    return lax.ppermute(value, "mp", [(0, 1), (1, 0)])


def from_axis(shard, count):
    return [shard] + [to_owner(shard, count - k, count) for k in range(1, count)]


def across(value, j, count):
    return lax.ppermute(value, "expert", [(e, e ^ j) for e in range(count)])


def sum_all(value):
    for axis in ("mp", "expert", "dp"):
        count, step = lax.axis_size(axis), 1
        while step < count:
            value = value + lax.ppermute(value, axis, [(i, i ^ step) for i in range(count)])
            step *= 2
    return value


def to_owner(chunk, k, count):
    return lax.ppermute(chunk, "dp", [(z, (z + k) % count) for z in range(count)])


def attend(project, bias, heads):
    images, seq = project.shape[0], project.shape[1]
    shape = (images, seq, heads, HEAD_DIM)
    width = heads * HEAD_DIM
    q = (project[:, :, :width] + bias[0]).astype(BF).reshape(shape)
    k = project[:, :, width : 2 * width].astype(BF).reshape(shape)
    v = (project[:, :, 2 * width :] + bias[1]).astype(BF).reshape(shape)
    scores = mm("iqhe,ikhe->ihqk", q, k) * HEAD_DIM ** (-0.5)
    probs = jax.nn.softmax(scores, axis=-1)
    mixed = mm("ihqk,ikhe->iqhe", probs.astype(BF), v).astype(BF)
    return (q, k, v, probs), mixed.reshape(images, seq, width)


def attend_back(kept, grad_mixed):
    q, k, v, probs = kept
    grad_mixed = grad_mixed.reshape(q.shape)
    scale = HEAD_DIM ** (-0.5)
    grad_v = mm("ihqk,iqhe->ikhe", probs.astype(BF), grad_mixed)
    grad_probs = mm("iqhe,ikhe->ihqk", grad_mixed, v)
    grad_scores = (
        probs * (grad_probs - jnp.sum(probs * grad_probs, axis=-1, keepdims=True))
    ).astype(BF)
    grad_q = mm("ihqk,ikhe->iqhe", grad_scores, k) * scale
    grad_k = mm("ihqk,iqhe->ikhe", grad_scores, q) * scale
    images, seq = q.shape[:2]
    return jnp.concatenate(
        [g.astype(BF).reshape(images, seq, -1) for g in (grad_q, grad_k, grad_v)], axis=-1
    )


def on_device(
    tokens, cotangent, routes, norm1_gain, norm1_shift, attn_input, input_bias, attn_output,
    output_bias, norm2_gain, norm2_shift, router_weight, up_weight, up_bias, down_weight, down_bias,
):
    rows, width = tokens.shape
    local = attn_input.shape[2]
    heads = local // HEAD_DIM
    mp_index, dp_index = lax.axis_index("mp"), lax.axis_index("dp")
    expert_index = lax.axis_index("expert")
    mp_count, dp_count = lax.axis_size("mp"), lax.axis_size("dp")
    expert_axis = lax.axis_size("expert")
    experts = router_weight.shape[1]
    capacity = 2 * rows // experts
    padded = -(-capacity // 8) * 8
    slots = experts * padded

    shard = jnp.concatenate(
        [attn_input.reshape(attn_input.shape[0], 3 * local), attn_output], axis=1
    )
    part = shard.shape[0] // expert_axis
    mine = lax.dynamic_slice_in_dim(shard, expert_index * part, part, 0)
    ff_part = up_weight.shape[2]
    bias_part = down_bias.shape[1]
    bias_own = jnp.concatenate([up_bias, down_bias], axis=1)
    bias_own = jnp.pad(bias_own, ((0, 7), (0, 4 * local - ff_part - bias_part)))
    column = jnp.stack(from_axis(jnp.concatenate([mine, bias_own]), dp_count))
    column = lax.dynamic_slice_in_dim(
        jnp.concatenate([column, column]), lax.rem(dp_count - dp_index, dp_count), dp_count, 0
    )
    up_bias_row = column[:, part, :ff_part].astype(F32).reshape(1, -1)
    down_bias_row = column[:, part, ff_part : ff_part + bias_part].astype(F32)
    column = column[:, :part]
    up_full = lax.all_gather(up_weight[0], "dp", axis=1, tiled=True)
    down_full = lax.all_gather(down_weight[0], "dp", axis=0, tiled=True)
    attn_full = jnp.zeros((dp_count, expert_axis) + mine.shape, BF)
    for j in range(expert_axis):
        piece = across(column, j, expert_axis) if j else column
        attn_full = lax.dynamic_update_slice(
            attn_full, piece[:, None], (0, expert_index ^ j, 0, 0)
        )
    attn_full = attn_full.reshape(width, 4 * local)
    input_full, output_full = attn_full[:, : 3 * local], attn_full[:, 3 * local :]

    other_tokens = swap(tokens)
    flat_routes = jnp.concatenate([routes[:, 0], routes[:, 1]])
    expert_ids = jnp.arange(experts, dtype=jnp.int32)
    one_hot = flat_routes[:, None] == expert_ids[None, :]
    order = jnp.arange(2 * rows, dtype=jnp.int32)
    before = (order[:, None] > order[None, :]).astype(BF)
    earlier = mm("ab,be->ae", before, one_hot.astype(BF))
    position = jnp.sum(jnp.where(one_hot, earlier, 0.0), axis=1).astype(jnp.int32)
    target = jnp.where(position < capacity, flat_routes * padded + position, slots)
    place = (target[:, None] == jnp.arange(slots, dtype=jnp.int32)[None, :]).astype(BF)
    place_both = place[:rows] + place[rows:]

    pair = jnp.stack([tokens, other_tokens]).astype(F32)
    xhat1, inverse1 = norm_stats(pair)
    normed = (xhat1 * norm1_gain + norm1_shift).astype(BF)
    local_bias = lax.dynamic_slice_in_dim(input_bias, mp_index * local, local, 1)
    project = mm("itd,df->itf", normed, input_full)
    kept, mixed_heads = attend(project, local_bias, heads)
    from_other = swap(mm("tf,df->td", mixed_heads[1], output_full))
    residual = (
        tokens.astype(F32) + mm("tf,df->td", mixed_heads[0], output_full) + from_other + output_bias
    )

    xhat2, inverse2 = norm_stats(residual)
    routed = (xhat2 * norm2_gain + norm2_shift).astype(BF)
    gates_all = jax.nn.softmax(mm("td,de->te", routed, router_weight), axis=-1)
    pick_first, pick_second = one_hot[:rows], one_hot[rows:]
    gate_first = jnp.sum(jnp.where(pick_first, gates_all, 0.0), axis=-1, keepdims=True)
    gate_second = jnp.sum(jnp.where(pick_second, gates_all, 0.0), axis=-1, keepdims=True)
    upstream = cotangent.astype(F32)
    route_grads = jnp.concatenate([gate_first * upstream, gate_second * upstream]).astype(BF)
    send = jnp.concatenate(
        [
            mm("ts,td->sd", place_both, routed).astype(BF),
            mm("ts,td->sd", place, route_grads).astype(BF),
        ],
        axis=1,
    ).reshape(experts, padded, 2 * width)
    received = lax.all_to_all(send, "expert", split_axis=0, concat_axis=0, tiled=True)
    received = received.reshape(-1, 2 * width)
    count = received.shape[0]
    both = jnp.concatenate([received, swap(received)], axis=0)
    slab, slab_grad = both[:, :width], both[:, width:]

    pre = mm("td,df->tf", slab, up_full) + up_bias_row
    cdf = 0.5 * (1.0 + lax.erf(pre * (0.5**0.5)))
    slope = cdf + pre * (jnp.exp(-0.5 * pre * pre) * 0.3989422804014327)
    hidden = (pre * cdf).astype(BF)
    bias_row = lax.dynamic_update_slice_in_dim(
        jnp.zeros((dp_count, mp_count, bias_part), F32), down_bias_row[:, None], mp_index, 1
    )
    produced = mm("tf,fd->td", hidden, down_full) + bias_row.reshape(1, -1)
    grad_pre = (mm("td,fd->tf", slab_grad, down_full) * slope).astype(BF)
    grad_slab = mm("tf,df->td", grad_pre, up_full)
    down_grad = mm("tf,td->fd", hidden, slab_grad).reshape(dp_count, ff_part, width)
    up_grad = mm("tf,td->fd", grad_pre, slab).reshape(dp_count, ff_part, width)
    column_sum = jnp.sum(slab_grad, axis=0, dtype=F32).reshape(dp_count, mp_count, bias_part)
    bias_grad = jnp.concatenate(
        [
            jnp.sum(grad_pre, axis=0, dtype=F32).reshape(dp_count, ff_part),
            lax.dynamic_index_in_dim(column_sum, mp_index, 1, keepdims=False),
        ],
        axis=1,
    )
    bias_grad = jnp.pad(
        bias_grad[:, None], ((0, 0), (0, 7), (0, width - ff_part - bias_part))
    )
    payload = jnp.concatenate([g.astype(BF) for g in (down_grad, up_grad, bias_grad)], axis=1)
    expert_grad = lax.psum_scatter(
        payload.reshape(-1, width), "dp", scatter_dimension=0, tiled=True
    ).astype(F32)
    partial = jnp.concatenate([produced, grad_slab], axis=1)
    back = (partial[:count] + swap(partial[count:].astype(BF)).astype(F32)).astype(BF)
    returned = lax.all_to_all(
        back.reshape(expert_axis, -1, 2 * width), "expert", split_axis=0, concat_axis=0, tiled=True
    ).reshape(slots, 2 * width)

    pick_one = mm("ts,sd->td", place[:rows], returned[:, :width])
    pick_two = mm("ts,sd->td", place[rows:], returned[:, :width])
    result = (residual + gate_first * pick_one + gate_second * pick_two).astype(BF)
    grad_first = jnp.sum(upstream * pick_one, axis=-1, keepdims=True)
    grad_second = jnp.sum(upstream * pick_two, axis=-1, keepdims=True)
    grad_gates = jnp.where(pick_first, grad_first, 0.0) + jnp.where(pick_second, grad_second, 0.0)
    grad_logits = gates_all * (grad_gates - jnp.sum(grad_gates * gates_all, axis=-1, keepdims=True))
    high = lax.Precision.HIGHEST
    router_grad = jnp.dot(routed.astype(F32).T, grad_logits, precision=high)
    grad_routed = jnp.dot(grad_logits, router_weight.astype(F32).T, precision=high)
    grad_routed = grad_routed + mm("ts,sd->td", place_both, returned[:, width:])
    grad_residual = upstream + norm_pull(xhat2, inverse2, norm2_gain, grad_routed)

    grad_branch = grad_residual.astype(BF)
    pair_grad = jnp.stack([grad_branch, swap(grad_branch)])
    grad_mixed = mm("itd,df->itf", pair_grad, output_full).astype(BF)
    output_grad = mm("itd,itf->df", pair_grad, mixed_heads)
    grad_project = attend_back(kept, grad_mixed)
    from_other = swap(mm("tf,df->td", grad_project[1], input_full).astype(BF))
    input_grad = mm("itd,itf->df", normed, grad_project)
    grad_normed = mm("tf,df->td", grad_project[0], input_full) + from_other.astype(F32)
    xhat_own, inverse_own = xhat1[0], inverse1[0]
    tokens_grad = grad_residual + norm_pull(xhat_own, inverse_own, norm1_gain, grad_normed)

    bias_local = jnp.sum(grad_project, axis=(0, 1), dtype=F32)
    bias_local = jnp.stack([bias_local[:local], bias_local[2 * local :]])
    bias_full = lax.dynamic_update_slice_in_dim(
        jnp.zeros((2, width), F32), bias_local, mp_index * local, 1
    )
    small = jnp.concatenate(
        [
            jnp.sum(grad_normed * xhat_own, axis=0)[None],
            jnp.sum(grad_normed, axis=0)[None],
            bias_full,
            jnp.sum(grad_residual, axis=0)[None],
            jnp.sum(grad_routed * xhat2, axis=0)[None],
            jnp.sum(grad_routed, axis=0)[None],
            router_grad.T,
        ]
    )
    attn_grad = jnp.concatenate([input_grad, output_grad], axis=1).astype(BF)
    attn_grad = attn_grad.reshape(dp_count, expert_axis, part, 4 * local)
    quarter = 0.0
    for j in range(expert_axis):
        piece = lax.dynamic_index_in_dim(attn_grad, expert_index ^ j, 1, keepdims=False)
        quarter = quarter + (across(piece, j, expert_axis) if j else piece).astype(F32)
    quarter = quarter.astype(BF)
    quarter, small = lax.optimization_barrier((quarter, small))
    share = 0.0
    for k in range(dp_count):
        piece = lax.dynamic_index_in_dim(
            quarter, lax.rem(dp_index + k, dp_count), 0, keepdims=False
        )
        share = share + (to_owner(piece, k, dp_count) if k else piece).astype(F32)
    share = share.astype(BF)
    attn_grad = jnp.zeros((expert_axis,) + share.shape, F32)
    for j in range(expert_axis):
        piece = (across(share, j, expert_axis) if j else share).astype(F32)
        attn_grad = lax.dynamic_update_slice(attn_grad, piece[None], (expert_index ^ j, 0, 0))
    attn_grad = attn_grad.reshape(-1, 4 * local)

    small = sum_all(small)
    bias_total = expert_grad[2 * ff_part :][:1]
    return (
        result,
        tokens_grad,
        small[0],
        small[1],
        attn_grad[:, : 3 * local].reshape(-1, 3, local),
        small[2:4],
        attn_grad[:, 3 * local :],
        small[4],
        small[5],
        small[6],
        small[7:].T,
        expert_grad[ff_part : 2 * ff_part].T[None],
        bias_total[:, :ff_part],
        expert_grad[None, :ff_part],
        bias_total[:, ff_part : ff_part + bias_part],
    )


def solution(mesh):
    token_spec = P(("expert", "dp", "mp"), None)
    return jax.shard_map(
        on_device,
        mesh=mesh,
        in_specs=(
            token_spec, token_spec, token_spec, P(), P(), P("dp", None, "mp"), P(), P("dp", "mp"),
            P(), P(), P(), P(), P("expert", None, ("dp", "mp")), P("expert", ("dp", "mp")),
            P("expert", ("dp", "mp"), None), P("expert", ("dp", "mp")),
        ),
        out_specs=(
            token_spec, token_spec, P(), P(), P("dp", None, "mp"), P(), P("dp", "mp"),
            P(), P(), P(), P(), P("expert", None, ("dp", "mp")), P("expert", ("dp", "mp")),
            P("expert", ("dp", "mp"), None), P("expert", ("dp", "mp")),
        ),
        check_vma=False,
    )
```
